128 devices in a mesh: depth: 4 (over z), row: 8 (over y, core), col: 4 (over x).
Axes of the slice: x: 4, y: 4, z: 4, core: 2. Of those that a mesh axis runs over, the one named last changes fastest.
Arguments:
- inputs: bfloat16 [1024, 12288], P(('depth', 'col'), 'row'), may hold values from -6 to 6
- w_in: bfloat16 [12288, 24576], P('row', ('depth', 'col')), may hold values from -0.0546875 to 0.0546875
- w_out: bfloat16 [24576, 12288], P(('depth', 'col'), 'row'), may hold values from -0.01953125 to 0.01953125
- out_grad: bfloat16 [1024, 12288], P(('depth', 'col'), 'row'), may hold values from -6 to 6
Outputs:
- outputs: bfloat16 [1024, 12288], P(('depth', 'col'), 'row')
- in_grad: bfloat16 [1024, 12288], P(('depth', 'col'), 'row')
The draws below stay inside these ranges and needn't reach their ends.
All inputs are finite; a program needn't handle non-finite values.
Results may differ from the reference program's by a relative error of at most 0.009.
Values may be sent and summed in bfloat16 or wider, within the bound.
No kernel may reach another device: no remote copies, remote signals or barrier semaphores. Data moves between devices by JAX's collectives and lax.ppermute only.
A program may use at most 128 MiB of HBM per device.

```python
import jax
import jax.numpy as jnp
from jax import lax

D = 12288
FF = 24576
TOKENS = 1024


def block_levels(own_key, extent, cuts, least, largest):
    def one(axis_at, parts):
        steps = jax.random.uniform(jax.random.fold_in(jax.random.fold_in(own_key, 6), axis_at), (parts,), jnp.float32, least / len(cuts), largest / len(cuts))
        return jnp.repeat(jnp.exp(steps), extent[axis_at] // parts).reshape((-1,) + (1,) * (len(extent) - axis_at - 1))

    gain = one(*cuts[0])
    for cut in cuts[1:]:
        gain = gain * one(*cut)
    return gain


def gaussian(rng, extent, scale, reach, shards=(), dtype=jnp.bfloat16):
    gain = block_levels(rng, extent, shards, -0.22, 0.18) if shards else 1.0
    result = jax.random.normal(rng, extent, jnp.float32) * scale * gain
    return jnp.minimum(jnp.maximum(result, -reach), reach).astype(dtype)


def setup_inputs(seed: int = 0) -> dict:
    arg_keys = jax.random.split(jax.random.key(seed), 5)
    inputs = gaussian(arg_keys[0], (TOKENS, D), 1.0, 6.0, ((0, 16), (1, 8)))
    w_in = gaussian(arg_keys[1], (D, FF), D ** -0.5, 0.0546875, ((0, 8), (1, 16)))
    w_out = gaussian(arg_keys[2], (FF, D), (4 * FF) ** -0.5, 0.01953125, ((0, 16), (1, 8)))
    out_grad = gaussian(arg_keys[3], (TOKENS, D), 1.0, 6.0, ((0, 16), (1, 8)))
    return dict(inputs=inputs, w_in=w_in, w_out=w_out, out_grad=out_grad)


curve = 0.7978845608028654
cubic = 0.044715


def gelu_value(value):
    tangent = jnp.tanh(curve * (value + cubic * value * value * value))
    return 0.5 * value * (1.0 + tangent)


def gelu_slope(value):
    tangent = jnp.tanh(curve * (value + cubic * value * value * value))
    return 0.5 * (1.0 + tangent) + 0.5 * value * (1.0 - tangent * tangent) * curve * (1.0 + 3.0 * cubic * value * value)


def reference(inputs, w_in, w_out, out_grad):
    pre = jnp.dot(inputs, w_in, preferred_element_type=jnp.float32)
    act = gelu_value(pre).astype(jnp.bfloat16)
    outputs = jnp.dot(act, w_out, preferred_element_type=jnp.float32).astype(jnp.bfloat16)
    grad_act = lax.dot_general(out_grad, w_out, (((1,), (1,)), ((), ())), preferred_element_type=jnp.float32)
    grad_pre = (grad_act * gelu_slope(pre)).astype(jnp.bfloat16)
    in_grad = lax.dot_general(grad_pre, w_in, (((1,), (1,)), ((), ())), preferred_element_type=jnp.float32).astype(jnp.bfloat16)
    return outputs, in_grad
```

```python
import functools

import jax
import jax.numpy as jnp
from jax import lax
from jax.experimental import pallas as pl
from jax.experimental.pallas import tpu as pltpu
from jax.sharding import PartitionSpec as P

curve = 0.7978845608028654
cubic = 0.044715
AXES = ("depth", "row", "col")
BLOCK = 64


def gelu_value(value):
    tangent = jnp.tanh(curve * (value + cubic * value * value * value))
    return 0.5 * value * (1.0 + tangent)


def gelu_slope(value):
    tangent = jnp.tanh(curve * (value + cubic * value * value * value))
    return 0.5 * (1.0 + tangent) + 0.5 * value * (1.0 - tangent * tangent) * curve * (
        1.0 + 3.0 * cubic * value * value
    )


def device_pairs(move):
    pairs = []
    for z in range(4):
        for r in range(8):
            for x in range(4):
                to_z, to_y, to_core, to_x = move(z, r // 2, r % 2, x)
                source = z * 32 + r * 4 + x
                target = (to_z % 4) * 32 + ((to_y % 4) * 2 + to_core) * 4 + to_x % 4
                pairs.append((source, target))
    return pairs


def send(value, move):
    return lax.ppermute(value, AXES, device_pairs(move))


def first_axis(k):
    return lambda z, y, core, x: (z + k * core, y, core, x + k * (1 - core))


def second_axis(k):
    return lambda z, y, core, x: (z + k * (1 - core), y, core, x + k * core)


def along_y(k):
    return lambda z, y, core, x: (z, y + k, core, x)


def other_core(z, y, core, x):
    return (z, y, 1 - core, x)


def matmul_kernel(place, transposed, counts, pieces, sizes, *refs):
    sources = refs[:pieces]
    weight = refs[pieces]
    outs = refs[pieces + 1 : -2]
    rows, arrived = refs[-2:]

    @pl.when(pl.program_id(0) == 0)
    def _():
        row = lax.axis_index("row")
        core, y = lax.rem(row, 2), lax.div(row, 2)
        copies = []
        for piece, source in enumerate(sources):
            for block in range(counts):
                at = pl.multiple_of(place(piece, block, core, y) * BLOCK, BLOCK)
                copies.append(
                    pltpu.make_async_copy(
                        source.at[pl.ds(block * BLOCK, BLOCK)],
                        rows.at[pl.ds(at, BLOCK)],
                        arrived.at[len(copies)],
                    )
                )
        for copy in copies:
            copy.start()
        for copy in copies:
            copy.wait()

    contract = 1 if transposed else 0
    product = lax.dot_general(
        rows[...],
        weight[...],
        (((1,), (contract,)), ((), ())),
        preferred_element_type=jnp.float32,
    ).astype(jnp.bfloat16)
    start = 0
    for out, size in zip(outs, sizes):
        out[...] = product[start : start + size]
        start += size


def matmul(sources, weight, transposed, place, sizes, tile=256):
    depth = weight.shape[1] if transposed else weight.shape[0]
    width = weight.shape[0] if transposed else weight.shape[1]
    total = sum(sizes)
    counts = sources[0].shape[0] // BLOCK
    if transposed:
        weight_spec = pl.BlockSpec((tile, depth), lambda j: (j, 0))
    else:
        weight_spec = pl.BlockSpec((depth, tile), lambda j: (0, j))
    return pl.pallas_call(
        functools.partial(matmul_kernel, place, transposed, counts, len(sources), sizes),
        grid=(width // tile,),
        out_shape=[jax.ShapeDtypeStruct((size, width), jnp.bfloat16) for size in sizes],
        in_specs=[pl.BlockSpec(memory_space=pl.ANY)] * len(sources) + [weight_spec],
        out_specs=[pl.BlockSpec((size, tile), lambda j: (0, j)) for size in sizes],
        scratch_shapes=[
            pltpu.VMEM((total, depth), jnp.bfloat16),
            pltpu.SemaphoreType.DMA((total // BLOCK,)),
        ],
        compiler_params=pltpu.CompilerParams(vmem_limit_bytes=24 * 2**20),
        cost_estimate=pl.CostEstimate(
            flops=2 * total * depth * width,
            bytes_accessed=2 * (total * depth + depth * width + total * width),
            transcendentals=0,
        ),
    )(*sources, weight)


def place_terms(piece, block, core, y):
    dz = jnp.where(core == 0, piece, block)
    dx = jnp.where(core == 0, block, piece)
    half, step = lax.div(dz, 2), lax.rem(dz, 2)
    kept = jnp.where(half == core, 1, 0)
    return kept * 8 + lax.rem(dx - y + 4, 4) * 2 + step


def place_sums(piece, block, core, y):
    half = core if piece < 4 else 1 - core
    dz = 2 * half + block
    dx = lax.rem(y + piece % 4, 4)
    return jnp.where(core == 0, dz * 4 + dx, dx * 4 + dz)


def gather_tokens(own):
    near = [own] + [send(own, first_axis(-k)) for k in (1, 2, 3)]
    line = jnp.concatenate(near)
    return [line] + [send(line, second_axis(-k)) for k in (1, 2, 3)]


def sum_parts(parts):
    total = parts[0].astype(jnp.float32)
    for part in parts[1:]:
        total = total + part.astype(jnp.float32)
    return total


def reduce_rows(passed, kept):
    both = sum_parts([kept, send(passed, other_core)]).astype(jnp.bfloat16)
    quarters = [both[k * 128 : (k + 1) * 128] for k in range(4)]
    return sum_parts([quarters[0]] + [send(quarters[k], along_y(k)) for k in (1, 2, 3)])


def gather_rows(own):
    mine = [own] + [send(own, along_y(-k)) for k in (1, 2, 3)]
    return mine + [send(part, other_core) for part in mine]


def reduce_tokens(groups):
    line = sum_parts([groups[0]] + [send(groups[k], second_axis(k)) for k in (1, 2, 3)])
    line = line.astype(jnp.bfloat16)
    blocks = [line[k * BLOCK : (k + 1) * BLOCK] for k in range(4)]
    total = sum_parts([blocks[0]] + [send(blocks[k], first_axis(k)) for k in (1, 2, 3)])
    return total.astype(jnp.bfloat16)


def shards(inputs, w_in, w_out, out_grad):
    pre = reduce_rows(*matmul(gather_tokens(inputs), w_in, False, place_terms, [512, 512]))
    grad_act = reduce_rows(*matmul(gather_tokens(out_grad), w_out, True, place_terms, [512, 512]))
    act = gelu_value(pre).astype(jnp.bfloat16)
    grad_pre = (grad_act * gelu_slope(pre)).astype(jnp.bfloat16)
    outputs = reduce_tokens(matmul(gather_rows(act), w_out, False, place_sums, [256] * 4))
    in_grad = reduce_tokens(matmul(gather_rows(grad_pre), w_in, True, place_sums, [256] * 4))
    return (outputs, in_grad)


def solution(mesh):
    in_specs = (
        P(("depth", "col"), "row"),
        P("row", ("depth", "col")),
        P(("depth", "col"), "row"),
        P(("depth", "col"), "row"),
    )
    out_specs = (P(("depth", "col"), "row"), P(("depth", "col"), "row"))
    return jax.shard_map(shards, mesh=mesh, in_specs=in_specs, out_specs=out_specs, check_vma=False)
```

```python
import functools

import jax
import jax.numpy as jnp
from jax import lax
from jax.experimental import pallas as pl
from jax.experimental.pallas import tpu as pltpu
from jax.sharding import PartitionSpec as P

curve = 0.7978845608028654
cubic = 0.044715
AXES = ("depth", "row", "col")
BLOCK = 64
LIGHT = pl.CostEstimate(flops=1, bytes_accessed=1, transcendentals=0)


def gelu_value(value):
    tangent = jnp.tanh(curve * (value + cubic * value * value * value))
    return 0.5 * value * (1.0 + tangent)


def gelu_slope(value):
    tangent = jnp.tanh(curve * (value + cubic * value * value * value))
    return 0.5 * (1.0 + tangent) + 0.5 * value * (1.0 - tangent * tangent) * curve * (
        1.0 + 3.0 * cubic * value * value
    )


def device_pairs(move):
    pairs = []
    for z in range(4):
        for r in range(8):
            for x in range(4):
                to_z, to_y, to_core, to_x = move(z, r // 2, r % 2, x)
                source = z * 32 + r * 4 + x
                target = (to_z % 4) * 32 + ((to_y % 4) * 2 + to_core) * 4 + to_x % 4
                pairs.append((source, target))
    return pairs


def send(value, move):
    return lax.ppermute(value, AXES, device_pairs(move))


def first_axis(k):
    return lambda z, y, core, x: (z + k * core, y, core, x + k * (1 - core))


def second_axis(k):
    return lambda z, y, core, x: (z + k * (1 - core), y, core, x + k * core)


def along_y(z, y, core, x):
    return (z, y + 1 - 2 * core, core, x)


def other_core(z, y, core, x):
    return (z, y, 1 - core, x)


def place_term(dz, dx, core, y):
    slot = lax.rem(dx - y + 4, 4)
    low = lax.div(dz, 2)
    owner = jnp.where(slot == 1, 0, jnp.where(slot == 3, 1, low))
    near = lax.rem(dz + 2 * owner, 4)
    index = jnp.where(lax.rem(slot, 2) == 1, near, 6 - slot + lax.rem(dz, 2))
    return jnp.where(owner == core, 8, 0) + index


def gathered(group, block):
    def place(core, y, z, x):
        dz = jnp.where(core == 0, group, block)
        dx = jnp.where(core == 0, block, group)
        return place_term(dz, dx, core, y)

    return place


def summed(dz, dx, core):
    return jnp.where(core == 0, dz * 4 + dx, dx * 4 + dz)


def own_rows(block):
    return lambda core, y, z, x: summed(lax.rem(block + 2 * core, 4), y, core)


def near_rows(block, other):
    def place(core, y, z, x):
        holder = 1 - core if other else core
        return summed(lax.rem(block + 2 * holder, 4), lax.rem(y + 3 + 2 * holder, 4), core)

    return place


def far_rows(block, other):
    def place(core, y, z, x):
        holder = 1 - core if other else core
        return summed(block + 2 * holder, lax.rem(y + 2, 4), core)

    return place


def load_kernel(source, out, arrived):
    copy = pltpu.make_async_copy(source, out, arrived)
    copy.start()
    copy.wait()


def load(value):
    return pl.pallas_call(
        load_kernel,
        out_shape=jax.ShapeDtypeStruct(value.shape, value.dtype),
        in_specs=[pl.BlockSpec(memory_space=pltpu.HBM)],
        out_specs=pl.BlockSpec(memory_space=pltpu.VMEM),
        scratch_shapes=[pltpu.SemaphoreType.DMA],
        compiler_params=pltpu.CompilerParams(vmem_limit_bytes=16 * 2**20),
        cost_estimate=LIGHT,
    )(value)


def matmul_kernel(transposed, places, formed_places, *refs):
    sources, weight = refs[: len(places)], refs[len(places)]
    formed, out = refs[len(places) + 1 : -1], refs[-1]
    row = lax.axis_index("row")
    where = (lax.rem(row, 2), lax.div(row, 2), lax.axis_index("depth"), lax.axis_index("col"))
    contract = 1 if transposed else 0

    def put(value, blocks):
        for n, place in enumerate(blocks):
            at = place if isinstance(place, int) else place(*where)
            out[pl.ds(pl.multiple_of(at * BLOCK, BLOCK), BLOCK)] = value[n * BLOCK : (n + 1) * BLOCK]

    def multiply(left, blocks):
        product = lax.dot_general(
            left,
            weight[...],
            (((1,), (contract,)), ((), ())),
            preferred_element_type=jnp.float32,
        ).astype(jnp.bfloat16)
        put(product, blocks)

    small, small_blocks = [], []
    for source, blocks in zip(sources, places):
        if len(blocks) < 4:
            small.append(source[...])
            small_blocks += blocks
        else:
            for first in range(0, len(blocks), 4):
                rows = slice(first * BLOCK, (first + 4) * BLOCK)
                multiply(source[rows], blocks[first : first + 4])
    if small:
        multiply(jnp.concatenate(small), small_blocks)
    for source, blocks in zip(formed, formed_places):
        for n in range(len(blocks)):
            put(source[n * BLOCK : (n + 1) * BLOCK], blocks[n : n + 1])


def matmul(sources, places, weight, transposed, formed=(), formed_places=()):
    depth = weight.shape[1] if transposed else weight.shape[0]
    width = weight.shape[0] if transposed else weight.shape[1]
    total = sum(source.shape[0] for source in sources)
    rows = total + sum(value.shape[0] for value in formed)
    return pl.pallas_call(
        functools.partial(matmul_kernel, transposed, places, formed_places),
        out_shape=jax.ShapeDtypeStruct((rows, width), jnp.bfloat16),
        in_specs=[pl.BlockSpec(memory_space=pltpu.VMEM)] * (len(sources) + 1 + len(formed)),
        out_specs=pl.BlockSpec(memory_space=pltpu.VMEM),
        compiler_params=pltpu.CompilerParams(vmem_limit_bytes=24 * 2**20),
        cost_estimate=LIGHT,
    )(*sources, weight, *formed)


def in_order(count):
    return list(range(count))


def after(value, *others):
    return lax.optimization_barrier((value, *others))[0]


def sum_parts(*parts):
    total = parts[0].astype(jnp.float32)
    for part in parts[1:]:
        total = total + part.astype(jnp.float32)
    return total


def rounded(*parts):
    return sum_parts(*parts).astype(jnp.bfloat16)


def cut(value, parts):
    size = value.shape[0] // parts
    return [value[k * size : (k + 1) * size] for k in range(parts)]


def gather_line(own):
    return jnp.concatenate([own] + [send(own, first_axis(-k)) for k in (1, 2, 3)])


def gather_tokens(line, weight, transposed):
    up, down = send(line, second_axis(-1)), send(line, second_axis(1))
    rest = [send(up[:128], second_axis(-1)), send(down[128:], second_axis(1))]
    early = matmul(
        [line, up, down], [in_order(4), [4, 5, 6, 7], [8, 9, 10, 11]], weight, transposed
    )
    late_places = [[gathered(2, n) for n in range(2)], [gathered(2, n) for n in range(2, 4)]]
    early_places = [gathered(k, n) for k in (0, 1, 3) for n in range(4)]
    return matmul(rest, late_places, weight, transposed, [early], [early_places]), up, down


def reduce_rows(terms):
    both = rounded(terms[512:], send(terms[:512], other_core))
    far = send(both[256:384], along_y)
    near = jnp.concatenate([rounded(both[:128], far), both[128:256]])
    arrived = send(near, along_y)
    mine = jnp.concatenate([rounded(arrived[:128], both[384:]), arrived[128:]])
    other = send(mine, other_core)
    return sum_parts(mine, jnp.concatenate([other[128:], other[:128]]))


def gather_rows(own, weight, transposed):
    near = send(own, along_y)
    far = send(near[:128], along_y)
    other_near = send(near, other_core)
    early = matmul([own, near], [in_order(4), [4, 5, 6, 7]], weight, transposed)
    other_far = send(far, other_core)
    return matmul(
        [other_near, far, other_far],
        [
            [near_rows(n, True) for n in range(4)],
            [far_rows(n, False) for n in range(2)],
            [far_rows(n, True) for n in range(2)],
        ],
        weight,
        transposed,
        [early],
        [[own_rows(n) for n in range(4)] + [near_rows(n, False) for n in range(4)]],
    )


def reduce_tokens(terms):
    parts = cut(terms, 4)
    up, down = send(parts[2][:128], second_axis(1)), send(parts[2][128:], second_axis(-1))
    one = jnp.concatenate([rounded(parts[1][:128], up), parts[1][128:]])
    three = jnp.concatenate([parts[3][:128], rounded(parts[3][128:], down)])
    line = rounded(parts[0], send(one, second_axis(1)), send(three, second_axis(-1)))
    blocks = cut(line, 4)
    return rounded(blocks[0], *[send(blocks[k], first_axis(k)) for k in (1, 2, 3)])


def shards(inputs, w_in, w_out, out_grad):
    line = gather_line(inputs)
    w_in = load(after(w_in, line))
    terms, up, down = gather_tokens(line, w_in, False)
    grad_line = gather_line(after(out_grad, line))
    w_out = load(after(w_out, w_in))
    grad_terms, _, _ = gather_tokens(after(grad_line, up, down), w_out, True)
    pre = reduce_rows(terms)
    grad_act = reduce_rows(grad_terms)
    act = gelu_value(pre).astype(jnp.bfloat16)
    grad_pre = (grad_act * gelu_slope(pre)).astype(jnp.bfloat16)
    outputs = reduce_tokens(gather_rows(act, w_out, False))
    in_grad = reduce_tokens(gather_rows(grad_pre, w_in, True))
    return (outputs, in_grad)


def solution(mesh):
    in_specs = (
        P(("depth", "col"), "row"),
        P("row", ("depth", "col")),
        P(("depth", "col"), "row"),
        P(("depth", "col"), "row"),
    )
    out_specs = (P(("depth", "col"), "row"), P(("depth", "col"), "row"))
    return jax.shard_map(shards, mesh=mesh, in_specs=in_specs, out_specs=out_specs, check_vma=False)
```

```python
import functools

import jax
import jax.numpy as jnp
from jax import lax
from jax.experimental import pallas as pl
from jax.experimental.pallas import tpu as pltpu
from jax.sharding import PartitionSpec as P

curve = 0.7978845608028654
cubic = 0.044715
AXES = ("depth", "row", "col")
BLOCK = 64
LIGHT = pl.CostEstimate(flops=1, bytes_accessed=1, transcendentals=0)


def gelu_value(value):
    tangent = jnp.tanh(curve * (value + cubic * value * value * value))
    return 0.5 * value * (1.0 + tangent)


def gelu_slope(value):
    tangent = jnp.tanh(curve * (value + cubic * value * value * value))
    return 0.5 * (1.0 + tangent) + 0.5 * value * (1.0 - tangent * tangent) * curve * (
        1.0 + 3.0 * cubic * value * value
    )


def device_pairs(move):
    pairs = []
    for z in range(4):
        for r in range(8):
            for x in range(4):
                to_z, to_y, to_core, to_x = move(z, r // 2, r % 2, x)
                source = z * 32 + r * 4 + x
                target = (to_z % 4) * 32 + ((to_y % 4) * 2 + to_core) * 4 + to_x % 4
                pairs.append((source, target))
    return pairs


def send(value, move):
    return lax.ppermute(value, AXES, device_pairs(move))


def first_axis(k):
    return lambda z, y, core, x: (z + k * core, y, core, x + k * (1 - core))


def second_axis(k):
    return lambda z, y, core, x: (z + k * (1 - core), y, core, x + k * core)


def along_y(z, y, core, x):
    return (z, y + 1 - 2 * core, core, x)


def other_core(z, y, core, x):
    return (z, y, 1 - core, x)


def place_term(dz, dx, core, y):
    slot = lax.rem(dx - y + 4, 4)
    low = lax.div(dz, 2)
    owner = jnp.where(slot == 1, 0, jnp.where(slot == 3, 1, low))
    near = lax.rem(dz + 2 * owner, 4)
    index = jnp.where(lax.rem(slot, 2) == 1, near, 6 - slot + lax.rem(dz, 2))
    return jnp.where(owner == core, 8, 0) + index


def gathered(group, block):
    def place(core, y, z, x):
        dz = jnp.where(core == 0, group, block)
        dx = jnp.where(core == 0, block, group)
        return place_term(dz, dx, core, y)

    return place


def summed(dz, dx, core):
    return jnp.where(core == 0, dz * 4 + dx, dx * 4 + dz)


def own_rows(block):
    return lambda core, y, z, x: summed(lax.rem(block + 2 * core, 4), y, core)


def near_rows(block, other):
    def place(core, y, z, x):
        holder = 1 - core if other else core
        return summed(lax.rem(block + 2 * holder, 4), lax.rem(y + 3 + 2 * holder, 4), core)

    return place


def far_rows(block, other):
    def place(core, y, z, x):
        holder = 1 - core if other else core
        return summed(block + 2 * holder, lax.rem(y + 2, 4), core)

    return place


def load_kernel(source, out, arrived):
    copy = pltpu.make_async_copy(source, out, arrived)
    copy.start()
    copy.wait()


def load(value):
    return pl.pallas_call(
        load_kernel,
        out_shape=jax.ShapeDtypeStruct(value.shape, value.dtype),
        in_specs=[pl.BlockSpec(memory_space=pltpu.HBM)],
        out_specs=pl.BlockSpec(memory_space=pltpu.VMEM),
        scratch_shapes=[pltpu.SemaphoreType.DMA],
        compiler_params=pltpu.CompilerParams(vmem_limit_bytes=16 * 2**20),
        cost_estimate=LIGHT,
    )(value)


def matmul_kernel(transposed, places, formed_places, *refs):
    sources, weight = refs[: len(places)], refs[len(places)]
    formed, out = refs[len(places) + 1 : -1], refs[-1]
    row = lax.axis_index("row")
    where = (lax.rem(row, 2), lax.div(row, 2), lax.axis_index("depth"), lax.axis_index("col"))
    contract = 1 if transposed else 0

    def put(value, blocks):
        for n, place in enumerate(blocks):
            at = place if isinstance(place, int) else place(*where)
            out[pl.ds(pl.multiple_of(at * BLOCK, BLOCK), BLOCK)] = value[n * BLOCK : (n + 1) * BLOCK]

    def multiply(left, blocks):
        product = lax.dot_general(
            left,
            weight[...],
            (((1,), (contract,)), ((), ())),
            preferred_element_type=jnp.float32,
        ).astype(jnp.bfloat16)
        put(product, blocks)

    small, small_blocks = [], []
    for source, blocks in zip(sources, places):
        if len(blocks) < 4:
            small.append(source[...])
            small_blocks += blocks
        else:
            for first in range(0, len(blocks), 4):
                rows = slice(first * BLOCK, (first + 4) * BLOCK)
                multiply(source[rows], blocks[first : first + 4])
    if small:
        multiply(jnp.concatenate(small), small_blocks)
    for source, blocks in zip(formed, formed_places):
        for n in range(len(blocks)):
            put(source[n * BLOCK : (n + 1) * BLOCK], blocks[n : n + 1])


def matmul(sources, places, weight, transposed, formed=(), formed_places=()):
    depth = weight.shape[1] if transposed else weight.shape[0]
    width = weight.shape[0] if transposed else weight.shape[1]
    total = sum(source.shape[0] for source in sources)
    rows = total + sum(value.shape[0] for value in formed)
    return pl.pallas_call(
        functools.partial(matmul_kernel, transposed, places, formed_places),
        out_shape=jax.ShapeDtypeStruct((rows, width), jnp.bfloat16),
        in_specs=[pl.BlockSpec(memory_space=pltpu.VMEM)] * (len(sources) + 1 + len(formed)),
        out_specs=pl.BlockSpec(memory_space=pltpu.VMEM),
        compiler_params=pltpu.CompilerParams(vmem_limit_bytes=24 * 2**20),
        cost_estimate=LIGHT,
    )(*sources, weight, *formed)


def in_order(count):
    return list(range(count))


def after(value, *others):
    return lax.optimization_barrier((value, *others))[0]


def sum_parts(*parts):
    total = parts[0].astype(jnp.float32)
    for part in parts[1:]:
        total = total + part.astype(jnp.float32)
    return total


def rounded(*parts):
    return sum_parts(*parts).astype(jnp.bfloat16)


def cut(value, parts):
    size = value.shape[0] // parts
    return [value[k * size : (k + 1) * size] for k in range(parts)]


def swap(value):
    if value.shape[0] < 512:
        return send(value, other_core)
    return jnp.concatenate([send(part, other_core) for part in cut(value, 2)])


def gather_lines(own, grad_own):
    both = jnp.concatenate([own, grad_own])
    parts = [send(both, first_axis(-k)) for k in (1, 2, 3)]
    line = jnp.concatenate([own] + [part[:BLOCK] for part in parts])
    return line, jnp.concatenate([grad_own] + [part[BLOCK:] for part in parts])


def ring(line):
    return send(line, second_axis(-1)), send(line, second_axis(1))


def ring_rest(up, down):
    return [send(up[:128], second_axis(-1)), send(down[128:], second_axis(1))]


def near_terms(line, up, down, weight, transposed):
    places = [in_order(4), [4, 5, 6, 7], [8, 9, 10, 11]]
    return matmul([line, up, down], places, weight, transposed)


def all_terms(rest, near, weight, transposed):
    rest_places = [[gathered(2, n) for n in range(2)], [gathered(2, n) for n in range(2, 4)]]
    near_places = [gathered(k, n) for k in (0, 1, 3) for n in range(4)]
    return matmul(rest, rest_places, weight, transposed, [near], [near_places])


def add_far(both, far):
    return jnp.concatenate([rounded(both[:128], far), both[128:256]])


def add_own(arrived, both):
    return jnp.concatenate([rounded(arrived[:128], both[384:]), arrived[128:]])


def add_other(mine, other):
    return sum_parts(mine, jnp.concatenate([other[128:], other[:128]]))


def early_sums(own, near, weight, transposed):
    return matmul([own, near], [in_order(4), [4, 5, 6, 7]], weight, transposed)


def all_sums(other_near, far, other_far, early, weight, transposed):
    return matmul(
        [other_near, far, other_far],
        [
            [near_rows(n, True) for n in range(4)],
            [far_rows(n, False) for n in range(2)],
            [far_rows(n, True) for n in range(2)],
        ],
        weight,
        transposed,
        [early],
        [[own_rows(n) for n in range(4)] + [near_rows(n, False) for n in range(4)]],
    )


def pass_far(parts):
    return send(parts[2][:128], second_axis(1)), send(parts[2][128:], second_axis(-1))


def pass_near(parts, up, down):
    one = jnp.concatenate([rounded(parts[1][:128], up), parts[1][128:]])
    three = jnp.concatenate([parts[3][:128], rounded(parts[3][128:], down)])
    return send(one, second_axis(1)), send(three, second_axis(-1))


def finish(line):
    blocks = cut(line, 4)
    return rounded(blocks[0], *[send(blocks[k], first_axis(k)) for k in (1, 2, 3)])


def shards(inputs, w_in, w_out, out_grad):
    line, grad_line = gather_lines(inputs, out_grad)
    up, down = ring(line)
    w_in = load(after(w_in, line))
    rest = ring_rest(after(up, w_in), after(down, w_in))
    grad_up, grad_down = ring(grad_line)
    near = near_terms(line, up, down, w_in, False)
    grad_up, grad_down = after(grad_up, near), after(grad_down, near)
    terms = all_terms(rest, near, w_in, False)
    w_out = load(after(w_out, w_in))
    both = rounded(terms[512:], swap(terms[:512]))
    far = send(both[256:384], along_y)
    grad_rest = ring_rest(grad_up, grad_down)
    grad_near = near_terms(grad_line, after(grad_up, terms), grad_down, w_out, True)
    grad_terms = all_terms(grad_rest, grad_near, w_out, True)
    arrived = send(add_far(both, far), along_y)
    grad_both = rounded(grad_terms[512:], swap(grad_terms[:512]))
    mine = add_own(arrived, both)
    grad_far = send(grad_both[256:384], along_y)
    grad_arrived = send(add_far(grad_both, grad_far), along_y)
    pre = add_other(mine, swap(mine))
    act, slope = lax.optimization_barrier((gelu_value(pre).astype(jnp.bfloat16), gelu_slope(pre)))
    grad_mine = add_own(grad_arrived, grad_both)
    act_near = send(act, along_y)
    grad_act = add_other(grad_mine, swap(grad_mine))
    grad_pre = (grad_act * slope).astype(jnp.bfloat16)
    grad_pre_near = send(grad_pre, along_y)
    act_far = send(act_near[:128], along_y)
    act_other_near = swap(act_near)
    early = early_sums(act, act_near, w_out, False)
    grad_pre_far = send(grad_pre_near[:128], along_y)
    grad_pre_other_near = swap(grad_pre_near)
    grad_early = early_sums(grad_pre, grad_pre_near, w_in, True)
    act_other_far = send(act_far, other_core)
    sums = all_sums(act_other_near, act_far, act_other_far, early, w_out, False)
    parts = cut(sums, 4)
    grad_pre_far = after(grad_pre_far, sums)
    grad_pre_other_far = send(grad_pre_far, other_core)
    outer = pass_far(parts)
    inner = pass_near(parts, *outer)
    grad_sums = all_sums(
        grad_pre_other_near, grad_pre_far, grad_pre_other_far, grad_early, w_in, True
    )
    out_line = rounded(parts[0], *inner)
    grad_parts = cut(grad_sums, 4)
    grad_outer = pass_far(grad_parts)
    outputs = finish(out_line)
    grad_inner = pass_near(grad_parts, *grad_outer)
    in_grad = finish(rounded(grad_parts[0], *grad_inner))
    return (outputs, in_grad)


def solution(mesh):
    in_specs = (
        P(("depth", "col"), "row"),
        P("row", ("depth", "col")),
        P(("depth", "col"), "row"),
        P(("depth", "col"), "row"),
    )
    out_specs = (P(("depth", "col"), "row"), P(("depth", "col"), "row"))
    return jax.shard_map(shards, mesh=mesh, in_specs=in_specs, out_specs=out_specs, check_vma=False)
```

```python
import functools

import jax
import jax.numpy as jnp
from jax import lax
from jax.experimental import pallas as pl
from jax.experimental.pallas import tpu as pltpu
from jax.sharding import PartitionSpec as P

curve = 0.7978845608028654
cubic = 0.044715
AXES = ("depth", "row", "col")
BLOCK = 64
LIGHT = pl.CostEstimate(flops=1, bytes_accessed=1, transcendentals=0)


def gelu_value(value):
    tangent = jnp.tanh(curve * (value + cubic * value * value * value))
    return 0.5 * value * (1.0 + tangent)


def gelu_slope(value):
    tangent = jnp.tanh(curve * (value + cubic * value * value * value))
    return 0.5 * (1.0 + tangent) + 0.5 * value * (1.0 - tangent * tangent) * curve * (
        1.0 + 3.0 * cubic * value * value
    )


def device_pairs(move):
    pairs = []
    for z in range(4):
        for r in range(8):
            for x in range(4):
                to_z, to_y, to_core, to_x = move(z, r // 2, r % 2, x)
                source = z * 32 + r * 4 + x
                target = (to_z % 4) * 32 + ((to_y % 4) * 2 + to_core) * 4 + to_x % 4
                pairs.append((source, target))
    return pairs


def send(value, move):
    return lax.ppermute(value, AXES, device_pairs(move))


def first_axis(k):
    return lambda z, y, core, x: (z + k * core, y, core, x + k * (1 - core))


def second_axis(k):
    return lambda z, y, core, x: (z + k * (1 - core), y, core, x + k * core)


def along_y(z, y, core, x):
    return (z, y + 1 - 2 * core, core, x)


def other_core(z, y, core, x):
    return (z, y, 1 - core, x)


def place_term(dz, dx, core, y):
    slot = lax.rem(dx - y + 4, 4)
    low = lax.div(dz, 2)
    owner = jnp.where(slot == 1, 0, jnp.where(slot == 3, 1, low))
    near = lax.rem(dz + 2 * owner, 4)
    index = jnp.where(lax.rem(slot, 2) == 1, near, 6 - slot + lax.rem(dz, 2))
    return jnp.where(owner == core, 8, 0) + index


def gathered(group, block):
    def place(core, y, z, x):
        dz = jnp.where(core == 0, group, block)
        dx = jnp.where(core == 0, block, group)
        return place_term(dz, dx, core, y)

    return place


def summed(dz, dx, core):
    return jnp.where(core == 0, dz * 4 + dx, dx * 4 + dz)


def own_rows(block):
    return lambda core, y, z, x: summed(lax.rem(block + 2 * core, 4), y, core)


def near_rows(block, other):
    def place(core, y, z, x):
        holder = 1 - core if other else core
        return summed(lax.rem(block + 2 * holder, 4), lax.rem(y + 3 + 2 * holder, 4), core)

    return place


def far_rows(block, other):
    def place(core, y, z, x):
        holder = 1 - core if other else core
        return summed(block + 2 * holder, lax.rem(y + 2, 4), core)

    return place


def load_kernel(source, out, arrived):
    copy = pltpu.make_async_copy(source, out, arrived)
    copy.start()
    copy.wait()


def load(value):
    return pl.pallas_call(
        load_kernel,
        out_shape=jax.ShapeDtypeStruct(value.shape, value.dtype),
        in_specs=[pl.BlockSpec(memory_space=pltpu.HBM)],
        out_specs=pl.BlockSpec(memory_space=pltpu.VMEM),
        scratch_shapes=[pltpu.SemaphoreType.DMA],
        compiler_params=pltpu.CompilerParams(vmem_limit_bytes=16 * 2**20),
        cost_estimate=LIGHT,
    )(value)


def matmul_kernel(transposed, places, formed_places, *refs):
    sources, weight = refs[: len(places)], refs[len(places)]
    formed, out = refs[len(places) + 1 : -1], refs[-1]
    row = lax.axis_index("row")
    where = (lax.rem(row, 2), lax.div(row, 2), lax.axis_index("depth"), lax.axis_index("col"))
    contract = 1 if transposed else 0

    def put(value, blocks):
        for n, place in enumerate(blocks):
            at = place if isinstance(place, int) else place(*where)
            out[pl.ds(pl.multiple_of(at * BLOCK, BLOCK), BLOCK)] = value[n * BLOCK : (n + 1) * BLOCK]

    def multiply(left, blocks):
        product = lax.dot_general(
            left,
            weight[...],
            (((1,), (contract,)), ((), ())),
            preferred_element_type=jnp.float32,
        ).astype(jnp.bfloat16)
        put(product, blocks)

    small, small_blocks = [], []
    for source, blocks in zip(sources, places):
        if len(blocks) < 4:
            small.append(source[...])
            small_blocks += blocks
        else:
            for first in range(0, len(blocks), 4):
                rows = slice(first * BLOCK, (first + 4) * BLOCK)
                multiply(source[rows], blocks[first : first + 4])
    if small:
        multiply(jnp.concatenate(small), small_blocks)
    for source, blocks in zip(formed, formed_places):
        for n in range(len(blocks)):
            put(source[n * BLOCK : (n + 1) * BLOCK], blocks[n : n + 1])


def matmul(sources, places, weight, transposed, formed=(), formed_places=()):
    depth = weight.shape[1] if transposed else weight.shape[0]
    width = weight.shape[0] if transposed else weight.shape[1]
    total = sum(source.shape[0] for source in sources)
    rows = total + sum(value.shape[0] for value in formed)
    return pl.pallas_call(
        functools.partial(matmul_kernel, transposed, places, formed_places),
        out_shape=jax.ShapeDtypeStruct((rows, width), jnp.bfloat16),
        in_specs=[pl.BlockSpec(memory_space=pltpu.VMEM)] * (len(sources) + 1 + len(formed)),
        out_specs=pl.BlockSpec(memory_space=pltpu.VMEM),
        compiler_params=pltpu.CompilerParams(vmem_limit_bytes=24 * 2**20),
        cost_estimate=LIGHT,
    )(*sources, weight, *formed)


def in_order(count):
    return list(range(count))


def after(value, *others):
    return lax.optimization_barrier((value, *others))[0]


def sum_parts(*parts):
    total = parts[0].astype(jnp.float32)
    for part in parts[1:]:
        total = total + part.astype(jnp.float32)
    return total


def rounded(*parts):
    return sum_parts(*parts).astype(jnp.bfloat16)


def cut(value, parts):
    size = value.shape[0] // parts
    return [value[k * size : (k + 1) * size] for k in range(parts)]


def swap(value):
    if value.shape[0] < 512:
        return send(value, other_core)
    return jnp.concatenate([send(part, other_core) for part in cut(value, 2)])


def gather_lines(own, grad_own):
    wide = [(0, BLOCK, 0), (0, 0, 0)]
    upper = lax.broadcasted_iota(jnp.int32, (2 * BLOCK, own.shape[1]), 0) < BLOCK
    zero = jnp.zeros((), own.dtype)
    both = jnp.where(
        upper, lax.pad(own, zero, wide), lax.pad(grad_own, zero, [(BLOCK, 0, 0), (0, 0, 0)])
    )
    up, down = send(both, first_axis(-1)), send(both, first_axis(1))
    far = send(own, first_axis(2))
    core = lax.rem(lax.axis_index("row"), 2)
    passed = jnp.where(core == 0, up[BLOCK:], down[BLOCK:])
    grad_far = send(passed, lambda z, y, core, x: (z + core, y, core, x - (1 - core)))
    line = jnp.concatenate([own, up[:BLOCK], far, down[:BLOCK]])
    return line, jnp.concatenate([grad_own, up[BLOCK:], grad_far, down[BLOCK:]])


def ring(line):
    return send(line, second_axis(-1)), send(line, second_axis(1))


def ring_rest(up, down):
    return [send(up[:128], second_axis(-1)), send(down[128:], second_axis(1))]


def near_terms(line, up, down, weight, transposed):
    places = [in_order(4), [4, 5, 6, 7], [8, 9, 10, 11]]
    return matmul([line, up, down], places, weight, transposed)


def all_terms(rest, near, weight, transposed):
    rest_places = [[gathered(2, n) for n in range(2)], [gathered(2, n) for n in range(2, 4)]]
    near_places = [gathered(k, n) for k in (0, 1, 3) for n in range(4)]
    return matmul(rest, rest_places, weight, transposed, [near], [near_places])


def add_far(both, far):
    return jnp.concatenate([rounded(both[:128], far), both[128:256]])


def add_own(arrived, both):
    return jnp.concatenate([rounded(arrived[:128], both[384:]), arrived[128:]])


def add_other(mine, other):
    return sum_parts(mine, jnp.concatenate([other[128:], other[:128]]))


def early_sums(own, near, weight, transposed):
    return matmul([own, near], [in_order(4), [4, 5, 6, 7]], weight, transposed)


def all_sums(other_near, far, other_far, early, weight, transposed):
    return matmul(
        [other_near, far, other_far],
        [
            [near_rows(n, True) for n in range(4)],
            [far_rows(n, False) for n in range(2)],
            [far_rows(n, True) for n in range(2)],
        ],
        weight,
        transposed,
        [early],
        [[own_rows(n) for n in range(4)] + [near_rows(n, False) for n in range(4)]],
    )


def pass_far(parts):
    return send(parts[2][:128], second_axis(1)), send(parts[2][128:], second_axis(-1))


def pass_near(parts, up, down):
    one = jnp.concatenate([rounded(parts[1][:128], up), parts[1][128:]])
    three = jnp.concatenate([parts[3][:128], rounded(parts[3][128:], down)])
    return send(one, second_axis(1)), send(three, second_axis(-1))


def finish(line):
    blocks = cut(line, 4)
    return rounded(blocks[0], *[send(blocks[k], first_axis(k)) for k in (1, 2, 3)])


def shards(inputs, w_in, w_out, out_grad):
    line, grad_line = gather_lines(inputs, out_grad)
    up, down = ring(line)
    w_in = load(after(w_in, line))
    rest = ring_rest(after(up, w_in), after(down, w_in))
    grad_up, grad_down = ring(grad_line)
    near = near_terms(line, up, down, w_in, False)
    grad_up, grad_down = after(grad_up, near), after(grad_down, near)
    terms = all_terms(rest, near, w_in, False)
    w_out = load(after(w_out, w_in))
    both = rounded(terms[512:], swap(terms[:512]))
    far = send(both[256:384], along_y)
    grad_rest = ring_rest(grad_up, grad_down)
    grad_near = near_terms(grad_line, after(grad_up, terms), grad_down, w_out, True)
    grad_terms = all_terms(grad_rest, grad_near, w_out, True)
    arrived = send(add_far(both, far), along_y)
    grad_both = rounded(grad_terms[512:], swap(grad_terms[:512]))
    mine = add_own(arrived, both)
    grad_far = send(grad_both[256:384], along_y)
    grad_arrived = send(add_far(grad_both, grad_far), along_y)
    pre = add_other(mine, jnp.concatenate([send(part, other_core) for part in cut(mine, 4)]))
    act, slope = lax.optimization_barrier((gelu_value(pre).astype(jnp.bfloat16), gelu_slope(pre)))
    grad_mine = add_own(after(grad_arrived, act), grad_both)
    act_near = send(act, along_y)
    grad_act = add_other(
        grad_mine, jnp.concatenate([send(part, other_core) for part in cut(grad_mine, 4)])
    )
    grad_pre = (grad_act * slope).astype(jnp.bfloat16)
    grad_pre_near = send(grad_pre, along_y)
    act_far = send(act_near[:128], along_y)
    act_other_near = swap(act_near)
    early = early_sums(act, act_near, w_out, False)
    grad_pre_near = after(grad_pre_near, early)
    grad_pre_far = send(grad_pre_near[:128], along_y)
    grad_pre_other_near = swap(grad_pre_near)
    grad_early = early_sums(grad_pre, grad_pre_near, w_in, True)
    act_other_far = send(act_far, other_core)
    sums = all_sums(act_other_near, act_far, act_other_far, early, w_out, False)
    parts = cut(sums, 4)
    grad_pre_far = after(grad_pre_far, sums)
    grad_pre_other_far = send(grad_pre_far, other_core)
    outer = pass_far(parts)
    inner = pass_near(parts, *outer)
    grad_sums = all_sums(
        grad_pre_other_near, grad_pre_far, grad_pre_other_far, grad_early, w_in, True
    )
    out_line = rounded(parts[0], *inner)
    grad_parts = cut(grad_sums, 4)
    grad_outer = pass_far(grad_parts)
    outputs = finish(out_line)
    grad_inner = pass_near(grad_parts, *grad_outer)
    in_grad = finish(rounded(grad_parts[0], *grad_inner))
    return (outputs, in_grad)


def solution(mesh):
    in_specs = (
        P(("depth", "col"), "row"),
        P("row", ("depth", "col")),
        P(("depth", "col"), "row"),
        P(("depth", "col"), "row"),
    )
    out_specs = (P(("depth", "col"), "row"), P(("depth", "col"), "row"))
    return jax.shard_map(shards, mesh=mesh, in_specs=in_specs, out_specs=out_specs, check_vma=False)
```

```python
import functools

import jax
import jax.numpy as jnp
from jax import lax
from jax.experimental import pallas as pl
from jax.experimental.pallas import tpu as pltpu
from jax.sharding import PartitionSpec as P

curve = 0.7978845608028654
cubic = 0.044715
AXES = ("depth", "row", "col")
BLOCK = 64
LIGHT = pl.CostEstimate(flops=1, bytes_accessed=1, transcendentals=0)


def gelu_value(value):
    tangent = jnp.tanh(curve * (value + cubic * value * value * value))
    return 0.5 * value * (1.0 + tangent)


def gelu_slope(value):
    tangent = jnp.tanh(curve * (value + cubic * value * value * value))
    return 0.5 * (1.0 + tangent) + 0.5 * value * (1.0 - tangent * tangent) * curve * (
        1.0 + 3.0 * cubic * value * value
    )


def device_pairs(move):
    pairs = []
    for z in range(4):
        for r in range(8):
            for x in range(4):
                to_z, to_y, to_core, to_x = move(z, r // 2, r % 2, x)
                source = z * 32 + r * 4 + x
                target = (to_z % 4) * 32 + ((to_y % 4) * 2 + to_core) * 4 + to_x % 4
                pairs.append((source, target))
    return pairs


def send(value, move):
    return lax.ppermute(value, AXES, device_pairs(move))


def first_axis(k):
    return lambda z, y, core, x: (z + k * core, y, core, x + k * (1 - core))


def second_axis(k):
    return lambda z, y, core, x: (z + k * (1 - core), y, core, x + k * core)


def along_y(z, y, core, x):
    return (z, y + 1 - 2 * core, core, x)


def other_core(z, y, core, x):
    return (z, y, 1 - core, x)


def place_term(dz, dx, core, y):
    slot = lax.rem(dx - y + 4, 4)
    low = lax.div(dz, 2)
    owner = jnp.where(slot == 1, 0, jnp.where(slot == 3, 1, low))
    near = lax.rem(dz + 2 * owner, 4)
    index = jnp.where(lax.rem(slot, 2) == 1, near, 6 - slot + lax.rem(dz, 2))
    return jnp.where(owner == core, 8, 0) + index


def gathered(group, block):
    def place(core, y, z, x):
        dz = jnp.where(core == 0, group, block)
        dx = jnp.where(core == 0, block, group)
        return place_term(dz, dx, core, y)

    return place


def summed(dz, dx, core):
    return jnp.where(core == 0, dz * 4 + dx, dx * 4 + dz)


def own_rows(block):
    return lambda core, y, z, x: summed(lax.rem(block + 2 * core, 4), y, core)


def near_rows(block, other):
    def place(core, y, z, x):
        holder = 1 - core if other else core
        return summed(lax.rem(block + 2 * holder, 4), lax.rem(y + 3 + 2 * holder, 4), core)

    return place


def far_rows(block, other):
    def place(core, y, z, x):
        holder = 1 - core if other else core
        return summed(block + 2 * holder, lax.rem(y + 2, 4), core)

    return place


def load_kernel(source, out, arrived):
    copy = pltpu.make_async_copy(source, out, arrived)
    copy.start()
    copy.wait()


def load(value):
    return pl.pallas_call(
        load_kernel,
        out_shape=jax.ShapeDtypeStruct(value.shape, value.dtype),
        in_specs=[pl.BlockSpec(memory_space=pltpu.HBM)],
        out_specs=pl.BlockSpec(memory_space=pltpu.VMEM),
        scratch_shapes=[pltpu.SemaphoreType.DMA],
        compiler_params=pltpu.CompilerParams(vmem_limit_bytes=16 * 2**20),
        cost_estimate=LIGHT,
    )(value)


def matmul_kernel(transposed, places, formed_places, *refs):
    sources, weight = refs[: len(places)], refs[len(places)]
    formed, out = refs[len(places) + 1 : -1], refs[-1]
    row = lax.axis_index("row")
    where = (lax.rem(row, 2), lax.div(row, 2), lax.axis_index("depth"), lax.axis_index("col"))
    contract = 1 if transposed else 0

    def put(value, blocks):
        for n, place in enumerate(blocks):
            at = place if isinstance(place, int) else place(*where)
            out[pl.ds(pl.multiple_of(at * BLOCK, BLOCK), BLOCK)] = value[n * BLOCK : (n + 1) * BLOCK]

    def multiply(left, blocks):
        product = lax.dot_general(
            left,
            weight[...],
            (((1,), (contract,)), ((), ())),
            preferred_element_type=jnp.float32,
        ).astype(jnp.bfloat16)
        put(product, blocks)

    small, small_blocks = [], []
    for source, blocks in zip(sources, places):
        if len(blocks) < 4:
            small.append(source[...])
            small_blocks += blocks
        else:
            for first in range(0, len(blocks), 4):
                rows = slice(first * BLOCK, (first + 4) * BLOCK)
                multiply(source[rows], blocks[first : first + 4])
    if small:
        multiply(jnp.concatenate(small), small_blocks)
    for source, blocks in zip(formed, formed_places):
        for n in range(len(blocks)):
            put(source[n * BLOCK : (n + 1) * BLOCK], blocks[n : n + 1])


def matmul(sources, places, weight, transposed, formed=(), formed_places=()):
    depth = weight.shape[1] if transposed else weight.shape[0]
    width = weight.shape[0] if transposed else weight.shape[1]
    total = sum(source.shape[0] for source in sources)
    rows = total + sum(value.shape[0] for value in formed)
    return pl.pallas_call(
        functools.partial(matmul_kernel, transposed, places, formed_places),
        out_shape=jax.ShapeDtypeStruct((rows, width), jnp.bfloat16),
        in_specs=[pl.BlockSpec(memory_space=pltpu.VMEM)] * (len(sources) + 1 + len(formed)),
        out_specs=pl.BlockSpec(memory_space=pltpu.VMEM),
        compiler_params=pltpu.CompilerParams(vmem_limit_bytes=24 * 2**20),
        cost_estimate=LIGHT,
    )(*sources, weight, *formed)


def in_order(count):
    return list(range(count))


def after(value, *others):
    return lax.optimization_barrier((value, *others))[0]


def sum_parts(*parts):
    total = parts[0].astype(jnp.float32)
    for part in parts[1:]:
        total = total + part.astype(jnp.float32)
    return total


def rounded(*parts):
    return sum_parts(*parts).astype(jnp.bfloat16)


def cut(value, parts):
    size = value.shape[0] // parts
    return [value[k * size : (k + 1) * size] for k in range(parts)]


def swap(value):
    if value.shape[0] < 512:
        return send(value, other_core)
    return jnp.concatenate([send(part, other_core) for part in cut(value, 2)])


def gather_lines(own, grad_own):
    wide = [(0, BLOCK, 0), (0, 0, 0)]
    upper = lax.broadcasted_iota(jnp.int32, (2 * BLOCK, own.shape[1]), 0) < BLOCK
    zero = jnp.zeros((), own.dtype)
    both = jnp.where(
        upper, lax.pad(own, zero, wide), lax.pad(grad_own, zero, [(BLOCK, 0, 0), (0, 0, 0)])
    )
    parts = [send(both, first_axis(-k)) for k in (1, 2, 3)]
    line = jnp.concatenate([own] + [part[:BLOCK] for part in parts])
    return line, jnp.concatenate([grad_own] + [part[BLOCK:] for part in parts])


def ring(line):
    return send(line, second_axis(-1)), send(line, second_axis(1))


def ring_rest(up, down):
    return [send(up[:128], second_axis(-1)), send(down[128:], second_axis(1))]


def near_terms(line, up, down, weight, transposed):
    places = [in_order(4), [4, 5, 6, 7], [8, 9, 10, 11]]
    return matmul([line, up, down], places, weight, transposed)


def all_terms(rest, near, weight, transposed):
    rest_places = [[gathered(2, n) for n in range(2)], [gathered(2, n) for n in range(2, 4)]]
    near_places = [gathered(k, n) for k in (0, 1, 3) for n in range(4)]
    return matmul(rest, rest_places, weight, transposed, [near], [near_places])


def add_far(both, far):
    return jnp.concatenate([rounded(both[:128], far), both[128:256]])


def add_own(arrived, both):
    return jnp.concatenate([rounded(arrived[:128], both[384:]), arrived[128:]])


def add_other(mine, other):
    return sum_parts(mine, jnp.concatenate([other[128:], other[:128]]))


def early_sums(own, near, weight, transposed):
    return matmul([own, near], [in_order(4), [4, 5, 6, 7]], weight, transposed)


def all_sums(other_near, far, other_far, early, weight, transposed):
    return matmul(
        [other_near, far, other_far],
        [
            [near_rows(n, True) for n in range(4)],
            [far_rows(n, False) for n in range(2)],
            [far_rows(n, True) for n in range(2)],
        ],
        weight,
        transposed,
        [early],
        [[own_rows(n) for n in range(4)] + [near_rows(n, False) for n in range(4)]],
    )


def pass_far(parts):
    return send(parts[2][:128], second_axis(1)), send(parts[2][128:], second_axis(-1))


def pass_near(parts, up, down):
    one = jnp.concatenate([rounded(parts[1][:128], up), parts[1][128:]])
    three = jnp.concatenate([parts[3][:128], rounded(parts[3][128:], down)])
    return send(one, second_axis(1)), send(three, second_axis(-1))


def finish(line):
    blocks = cut(line, 4)
    return rounded(blocks[0], *[send(blocks[k], first_axis(k)) for k in (1, 2, 3)])


def shards(inputs, w_in, w_out, out_grad):
    line, grad_line = gather_lines(inputs, out_grad)
    up, down = ring(line)
    w_in = load(after(w_in, line))
    rest = ring_rest(after(up, w_in), after(down, w_in))
    grad_up, grad_down = ring(grad_line)
    near = near_terms(line, up, down, w_in, False)
    grad_up, grad_down = after(grad_up, near), after(grad_down, near)
    terms = all_terms(rest, near, w_in, False)
    w_out = load(after(w_out, w_in))
    both = rounded(terms[512:], swap(terms[:512]))
    far = send(both[256:384], along_y)
    grad_rest = ring_rest(grad_up, grad_down)
    grad_near = near_terms(grad_line, after(grad_up, terms), grad_down, w_out, True)
    grad_terms = all_terms(grad_rest, grad_near, w_out, True)
    arrived = send(add_far(both, far), along_y)
    grad_both = rounded(grad_terms[512:], swap(grad_terms[:512]))
    mine = add_own(arrived, both)
    grad_far = send(grad_both[256:384], along_y)
    grad_arrived = send(add_far(grad_both, grad_far), along_y)
    pre = add_other(mine, swap(mine))
    act, slope = lax.optimization_barrier((gelu_value(pre).astype(jnp.bfloat16), gelu_slope(pre)))
    grad_mine = add_own(grad_arrived, grad_both)
    act_near = send(act, along_y)
    grad_act = add_other(grad_mine, swap(grad_mine))
    grad_pre = (grad_act * slope).astype(jnp.bfloat16)
    grad_pre_near = send(grad_pre, along_y)
    act_far = send(act_near[:128], along_y)
    act_other_near = swap(act_near)
    early = early_sums(act, act_near, w_out, False)
    grad_pre_far = send(grad_pre_near[:128], along_y)
    grad_pre_other_near = swap(grad_pre_near)
    grad_early = early_sums(grad_pre, grad_pre_near, w_in, True)
    act_other_far = send(act_far, other_core)
    sums = all_sums(act_other_near, act_far, act_other_far, early, w_out, False)
    parts = cut(sums, 4)
    grad_pre_far = after(grad_pre_far, sums)
    grad_pre_other_far = send(grad_pre_far, other_core)
    outer = pass_far(parts)
    inner = pass_near(parts, *outer)
    grad_sums = all_sums(
        grad_pre_other_near, grad_pre_far, grad_pre_other_far, grad_early, w_in, True
    )
    out_line = rounded(parts[0], *inner)
    grad_parts = cut(grad_sums, 4)
    grad_outer = pass_far(grad_parts)
    outputs = finish(out_line)
    grad_inner = pass_near(grad_parts, *grad_outer)
    in_grad = finish(rounded(grad_parts[0], *grad_inner))
    return (outputs, in_grad)


def solution(mesh):
    in_specs = (
        P(("depth", "col"), "row"),
        P("row", ("depth", "col")),
        P(("depth", "col"), "row"),
        P(("depth", "col"), "row"),
    )
    out_specs = (P(("depth", "col"), "row"), P(("depth", "col"), "row"))
    return jax.shard_map(shards, mesh=mesh, in_specs=in_specs, out_specs=out_specs, check_vma=False)
```

```python
import functools

import jax
import jax.numpy as jnp
from jax import lax
from jax.experimental import pallas as pl
from jax.experimental.pallas import tpu as pltpu
from jax.sharding import PartitionSpec as P

curve = 0.7978845608028654
cubic = 0.044715
AXES = ("depth", "row", "col")
BLOCK = 64
LIGHT = pl.CostEstimate(flops=1, bytes_accessed=1, transcendentals=0)


def gelu_value(value):
    tangent = jnp.tanh(curve * (value + cubic * value * value * value))
    return 0.5 * value * (1.0 + tangent)


def gelu_slope(value):
    tangent = jnp.tanh(curve * (value + cubic * value * value * value))
    return 0.5 * (1.0 + tangent) + 0.5 * value * (1.0 - tangent * tangent) * curve * (
        1.0 + 3.0 * cubic * value * value
    )


def device_pairs(move):
    pairs = []
    for z in range(4):
        for r in range(8):
            for x in range(4):
                to_z, to_y, to_core, to_x = move(z, r // 2, r % 2, x)
                source = z * 32 + r * 4 + x
                target = (to_z % 4) * 32 + ((to_y % 4) * 2 + to_core) * 4 + to_x % 4
                pairs.append((source, target))
    return pairs


def send(value, move):
    return lax.ppermute(value, AXES, device_pairs(move))


def first_axis(k):
    return lambda z, y, core, x: (z + k * core, y, core, x + k * (1 - core))


def second_axis(k):
    return lambda z, y, core, x: (z + k * (1 - core), y, core, x + k * core)


def along_y(z, y, core, x):
    return (z, y + 1 - 2 * core, core, x)


def other_core(z, y, core, x):
    return (z, y, 1 - core, x)


def place_term(dz, dx, core, y):
    slot = lax.rem(dx - y + 4, 4)
    low = lax.div(dz, 2)
    owner = jnp.where(slot == 1, 0, jnp.where(slot == 3, 1, low))
    near = lax.rem(dz + 2 * owner, 4)
    index = jnp.where(lax.rem(slot, 2) == 1, near, 6 - slot + lax.rem(dz, 2))
    return jnp.where(owner == core, 8, 0) + index


def gathered(group, block):
    def place(core, y, z, x):
        dz = jnp.where(core == 0, group, block)
        dx = jnp.where(core == 0, block, group)
        return place_term(dz, dx, core, y)

    return place


def summed(dz, dx, core):
    return jnp.where(core == 0, dz * 4 + dx, dx * 4 + dz)


def own_rows(block):
    return lambda core, y, z, x: summed(lax.rem(block + 2 * core, 4), y, core)


def near_rows(block, other):
    def place(core, y, z, x):
        holder = 1 - core if other else core
        return summed(lax.rem(block + 2 * holder, 4), lax.rem(y + 3 + 2 * holder, 4), core)

    return place


def far_rows(block, other):
    def place(core, y, z, x):
        holder = 1 - core if other else core
        return summed(block + 2 * holder, lax.rem(y + 2, 4), core)

    return place


def load_kernel(source, out, arrived):
    copy = pltpu.make_async_copy(source, out, arrived)
    copy.start()
    copy.wait()


def load(value):
    return pl.pallas_call(
        load_kernel,
        out_shape=jax.ShapeDtypeStruct(value.shape, value.dtype),
        in_specs=[pl.BlockSpec(memory_space=pltpu.HBM)],
        out_specs=pl.BlockSpec(memory_space=pltpu.VMEM),
        scratch_shapes=[pltpu.SemaphoreType.DMA],
        compiler_params=pltpu.CompilerParams(vmem_limit_bytes=16 * 2**20),
        cost_estimate=LIGHT,
    )(value)


def matmul_kernel(transposed, places, formed_places, *refs):
    sources, weight = refs[: len(places)], refs[len(places)]
    formed, out = refs[len(places) + 1 : -1], refs[-1]
    row = lax.axis_index("row")
    where = (lax.rem(row, 2), lax.div(row, 2), lax.axis_index("depth"), lax.axis_index("col"))
    contract = 1 if transposed else 0

    def put(value, blocks):
        for n, place in enumerate(blocks):
            at = place if isinstance(place, int) else place(*where)
            out[pl.ds(pl.multiple_of(at * BLOCK, BLOCK), BLOCK)] = value[n * BLOCK : (n + 1) * BLOCK]

    def multiply(left, blocks):
        product = lax.dot_general(
            left,
            weight[...],
            (((1,), (contract,)), ((), ())),
            preferred_element_type=jnp.float32,
        ).astype(jnp.bfloat16)
        put(product, blocks)

    small, small_blocks = [], []
    for source, blocks in zip(sources, places):
        if len(blocks) < 4:
            small.append(source[...])
            small_blocks += blocks
        else:
            for first in range(0, len(blocks), 4):
                rows = slice(first * BLOCK, (first + 4) * BLOCK)
                multiply(source[rows], blocks[first : first + 4])
    if small:
        multiply(jnp.concatenate(small), small_blocks)
    for source, blocks in zip(formed, formed_places):
        for n in range(len(blocks)):
            put(source[n * BLOCK : (n + 1) * BLOCK], blocks[n : n + 1])


def matmul(sources, places, weight, transposed, formed=(), formed_places=()):
    depth = weight.shape[1] if transposed else weight.shape[0]
    width = weight.shape[0] if transposed else weight.shape[1]
    total = sum(source.shape[0] for source in sources)
    rows = total + sum(value.shape[0] for value in formed)
    return pl.pallas_call(
        functools.partial(matmul_kernel, transposed, places, formed_places),
        out_shape=jax.ShapeDtypeStruct((rows, width), jnp.bfloat16),
        in_specs=[pl.BlockSpec(memory_space=pltpu.VMEM)] * (len(sources) + 1 + len(formed)),
        out_specs=pl.BlockSpec(memory_space=pltpu.VMEM),
        compiler_params=pltpu.CompilerParams(vmem_limit_bytes=24 * 2**20),
        cost_estimate=LIGHT,
    )(*sources, weight, *formed)


def in_order(count):
    return list(range(count))


def after(value, *others):
    return lax.optimization_barrier((value, *others))[0]


def sum_parts(*parts):
    total = parts[0].astype(jnp.float32)
    for part in parts[1:]:
        total = total + part.astype(jnp.float32)
    return total


def rounded(*parts):
    return sum_parts(*parts).astype(jnp.bfloat16)


def cut(value, parts):
    size = value.shape[0] // parts
    return [value[k * size : (k + 1) * size] for k in range(parts)]


def swap(value):
    if value.shape[0] < 512:
        return send(value, other_core)
    return jnp.concatenate([send(part, other_core) for part in cut(value, 2)])


def gather_lines(own, grad_own):
    wide = [(0, BLOCK, 0), (0, 0, 0)]
    upper = lax.broadcasted_iota(jnp.int32, (2 * BLOCK, own.shape[1]), 0) < BLOCK
    zero = jnp.zeros((), own.dtype)
    both = jnp.where(
        upper, lax.pad(own, zero, wide), lax.pad(grad_own, zero, [(BLOCK, 0, 0), (0, 0, 0)])
    )
    parts = [send(both, first_axis(-k)) for k in (1, 2, 3)]
    line = jnp.concatenate([own] + [part[:BLOCK] for part in parts])
    return line, jnp.concatenate([grad_own] + [part[BLOCK:] for part in parts])


def ring(line):
    return send(line, second_axis(-1)), send(line, second_axis(1))


def ring_rest(up, down):
    return [send(up[:128], second_axis(-1)), send(down[128:], second_axis(1))]


def near_terms(line, up, down, weight, transposed):
    places = [in_order(4), [4, 5, 6, 7], [8, 9, 10, 11]]
    return matmul([line, up, down], places, weight, transposed)


def all_terms(rest, near, weight, transposed):
    rest_places = [[gathered(2, n) for n in range(2)], [gathered(2, n) for n in range(2, 4)]]
    near_places = [gathered(k, n) for k in (0, 1, 3) for n in range(4)]
    return matmul(rest, rest_places, weight, transposed, [near], [near_places])


def add_far(both, far):
    return jnp.concatenate([rounded(both[:128], far), both[128:256]])


def add_own(arrived, both):
    return jnp.concatenate([rounded(arrived[:128], both[384:]), arrived[128:]])


def add_other(mine, other):
    return sum_parts(mine, jnp.concatenate([other[128:], other[:128]]))


def early_sums(own, near, weight, transposed):
    return matmul([own, near], [in_order(4), [4, 5, 6, 7]], weight, transposed)


def all_sums(other_near, far, other_far, early, weight, transposed):
    return matmul(
        [other_near, far, other_far],
        [
            [near_rows(n, True) for n in range(4)],
            [far_rows(n, False) for n in range(2)],
            [far_rows(n, True) for n in range(2)],
        ],
        weight,
        transposed,
        [early],
        [[own_rows(n) for n in range(4)] + [near_rows(n, False) for n in range(4)]],
    )


def pass_far(parts):
    return send(parts[2][:128], second_axis(1)), send(parts[2][128:], second_axis(-1))


def pass_near(parts, up, down):
    one = jnp.concatenate([rounded(parts[1][:128], up), parts[1][128:]])
    three = jnp.concatenate([parts[3][:128], rounded(parts[3][128:], down)])
    return send(one, second_axis(1)), send(three, second_axis(-1))


def finish(line):
    blocks = cut(line, 4)
    return rounded(blocks[0], *[send(blocks[k], first_axis(k)) for k in (1, 2, 3)])


def shards(inputs, w_in, w_out, out_grad):
    line, grad_line = gather_lines(inputs, out_grad)
    up, down = ring(line)
    w_in = load(after(w_in, line))
    rest = ring_rest(after(up, w_in), after(down, w_in))
    grad_up, grad_down = ring(grad_line)
    near = near_terms(line, up, down, w_in, False)
    grad_up, grad_down = after(grad_up, near), after(grad_down, near)
    terms = all_terms(rest, near, w_in, False)
    w_out = load(after(w_out, w_in))
    both = rounded(terms[512:], swap(terms[:512]))
    far = send(both[256:384], along_y)
    grad_rest = ring_rest(grad_up, grad_down)
    grad_near = near_terms(grad_line, after(grad_up, terms), grad_down, w_out, True)
    grad_terms = all_terms(grad_rest, grad_near, w_out, True)
    arrived = send(add_far(both, far), along_y)
    grad_both = rounded(grad_terms[512:], swap(grad_terms[:512]))
    mine = add_own(arrived, both)
    grad_far = send(grad_both[256:384], along_y)
    grad_arrived = send(add_far(grad_both, grad_far), along_y)
    pre = add_other(mine, jnp.concatenate([send(part, other_core) for part in cut(mine, 4)]))
    act, slope = lax.optimization_barrier((gelu_value(pre).astype(jnp.bfloat16), gelu_slope(pre)))
    grad_mine = add_own(after(grad_arrived, act), grad_both)
    act_near = send(act, along_y)
    grad_act = add_other(grad_mine, swap(grad_mine))
    grad_pre = (grad_act * slope).astype(jnp.bfloat16)
    grad_pre_near = send(grad_pre, along_y)
    act_far = send(act_near[:128], along_y)
    act_other_near = swap(act_near)
    early = early_sums(act, act_near, w_out, False)
    grad_pre_far = send(grad_pre_near[:128], along_y)
    grad_pre_other_near = swap(grad_pre_near)
    grad_early = early_sums(grad_pre, grad_pre_near, w_in, True)
    act_other_far = send(act_far, other_core)
    sums = all_sums(act_other_near, act_far, act_other_far, early, w_out, False)
    parts = cut(sums, 4)
    grad_pre_far = after(grad_pre_far, sums)
    grad_pre_other_far = send(grad_pre_far, other_core)
    outer = pass_far(parts)
    inner = pass_near(parts, *outer)
    grad_sums = all_sums(
        grad_pre_other_near, grad_pre_far, grad_pre_other_far, grad_early, w_in, True
    )
    out_line = rounded(parts[0], *inner)
    grad_parts = cut(grad_sums, 4)
    grad_outer = pass_far(grad_parts)
    outputs = finish(out_line)
    grad_inner = pass_near(grad_parts, *grad_outer)
    in_grad = finish(rounded(grad_parts[0], *grad_inner))
    return (outputs, in_grad)


def solution(mesh):
    in_specs = (
        P(("depth", "col"), "row"),
        P("row", ("depth", "col")),
        P(("depth", "col"), "row"),
        P(("depth", "col"), "row"),
    )
    out_specs = (P(("depth", "col"), "row"), P(("depth", "col"), "row"))
    return jax.shard_map(shards, mesh=mesh, in_specs=in_specs, out_specs=out_specs, check_vma=False)
```
